512 devices in a mesh: blk: 32 (over y, z_lo, core), pw: 16 (over x, z_hi).
Axes of the slice: x: 4, y: 4, z: 16 (z_hi: 4, z_lo: 4; z = z_hi * 4 + z_lo), core: 2. Of those that a mesh axis runs over, the one named last changes fastest.
Arguments:
- res_pair: bfloat16 [65536, 12288], P('blk', 'pw'), may hold values from -0.56640625 to 0.56640625
- band_pair: bfloat16 [8192, 12288], P('blk', 'pw'), may hold values from -0.56640625 to 0.56640625
- coulomb: float32 [12288], P('pw'), may hold values from 0.2 to 5
- screening: float32 [2048], P('pw'), may hold values from 0.2 to 5
- val_form: bfloat16 [400, 2048], P(None, 'pw'), may hold values from -2.3125 to 2.3125
- cond_form: bfloat16 [600, 2048], P(None, 'pw'), may hold values from -2.3125 to 2.3125
- res_bands: int32 [3, 65536], P(None, 'blk'), may hold values from 0 to 299, as said below
- band_bands: int32 [3, 8192], P(None, 'blk'), may hold values from 0 to 299, as said below
Outputs:
- kernel: float32 [2, 65536, 256], P(None, ('blk', 'pw'))
The draws below stay inside these ranges and needn't reach their ends.
Inputs may be any that keep to these rules, and one draw needn't show every extreme that they name: `res_bands`: row 0 holds valence bands below 200, row 1 conduction bands below 300, row 2 k-points below 2. `band_bands`: row 0 holds valence bands below 200, row 1 conduction bands below 300, row 2 k-points below 2.
All inputs are finite; a program needn't handle non-finite values.
Results may differ from the reference program's by a relative error of at most 0.01.
Values may be sent and summed in bfloat16 or wider, within the bound.
No kernel may reach another device: no remote copies, remote signals or barrier semaphores. Data moves between devices by JAX's collectives and lax.ppermute only.
A program may use at most 64 MiB of HBM per device.

```python
import math
import jax
import jax.numpy as jnp
from jax import lax

NPW = 12288
NGW = 2048
NV = 200
NC = 300
NK = 2
RES = 2048
VB = 256
STEPS = 2
TRANS = 65536
BAND = 8192
N_BLK = 32
N_PW = 16


def draw_bands(key, count):
    first, second, third = jax.random.split(key, 3)
    valence = jax.random.randint(first, (count,), 0, NV, dtype=jnp.int32)
    conduct = jax.random.randint(second, (count,), 0, NC, dtype=jnp.int32)
    kpoint = jax.random.randint(third, (count,), 0, NK, dtype=jnp.int32)
    return jnp.stack([valence, conduct, kpoint], axis=0)


def draw_res_bands(key, part):
    key = jax.random.fold_in(key, 11)
    return draw_bands(key, TRANS)


def draw_band_bands(key, part):
    key = jax.random.fold_in(key, 23)
    return draw_bands(key, BAND)


def steps_of(rng, dims, cuts, least, largest):
    loudness = 1.0
    for dim, blocks in cuts:
        draws = jax.random.uniform(jax.random.fold_in(jax.random.fold_in(rng, 6), dim), (blocks,), jnp.float32, least / len(cuts), largest / len(cuts))
        loudness = loudness * jnp.repeat(jnp.exp(draws), dims[dim] // blocks).reshape((-1,) + (1,) * (len(dims) - 1 - dim))
    return loudness


def bell_draw(key, extent, deviation, most, cuts=(), kind=jnp.bfloat16):
    level = steps_of(key, extent, cuts, -0.22, 0.18) if cuts else 1.0
    drawn = jax.random.normal(key, extent, jnp.float32) * deviation * level
    return jnp.minimum(jnp.maximum(drawn, -most), most).astype(kind)


def setup_inputs(seed: int = 0) -> dict:
    key_of = jax.random.split(jax.random.key(seed), 9)
    return {
        "res_pair": bell_draw(key_of[0], (TRANS, NPW), (NPW ** -0.25), 0.56640625, ((0, 32), (1, 16))),
        "band_pair": bell_draw(key_of[1], (BAND, NPW), (NPW ** -0.25), 0.56640625, ((0, 32), (1, 16))),
        "coulomb": jnp.clip(jnp.exp(math.log(5.0) - 3.218876 * jax.random.uniform(key_of[2], (NPW,), jnp.float32) ** steps_of(key_of[2], (NPW,), ((0, 16),), -0.2, 0.2)), 0.2, 5.0),
        "screening": jnp.clip(jnp.exp(math.log(5.0) - 3.218876 * jax.random.uniform(key_of[3], (NGW,), jnp.float32) ** steps_of(key_of[3], (NGW,), ((0, 16),), -0.2, 0.2)), 0.2, 5.0),
        "val_form": bell_draw(key_of[4], (NK * NV, NGW), (NGW ** -0.125), 2.3125, ((1, 16),)),
        "cond_form": bell_draw(key_of[5], (NK * NC, NGW), (NGW ** -0.125), 2.3125, ((1, 16),)),
        "res_bands": draw_res_bands(jax.random.fold_in(key_of[8], 71), 0),
        "band_bands": draw_band_bands(jax.random.fold_in(key_of[8], 71), 0),
    }


def make_density(bands, val_form, cond_form):
    rows_val = bands[2] * NV + bands[0]
    rows_cond = bands[2] * NC + bands[1]
    valence = jnp.take(val_form, rows_val.astype(jnp.int32), axis=0).astype(jnp.float32)
    conduct = jnp.take(cond_form, rows_cond.astype(jnp.int32), axis=0).astype(jnp.float32)
    return (valence * conduct).astype(jnp.bfloat16)


def reference(res_pair, band_pair, coulomb, screening, val_form, cond_form, res_bands, band_bands):
    highest = lax.Precision.HIGHEST
    res_density = make_density(res_bands, val_form, cond_form)
    band_density = make_density(band_bands, val_form, cond_form)
    weighted = (band_pair.astype(jnp.float32) * coulomb[None, :]).astype(jnp.bfloat16)
    screened = (band_density.astype(jnp.float32) * screening[None, :]).astype(jnp.bfloat16)
    pair_groups = NPW // N_PW
    screen_groups = NGW // N_PW

    def one_block(block_index):
        start = (block_index * RES).astype(jnp.int32)
        pair_rows = lax.dynamic_slice_in_dim(res_pair, start, RES, 0).astype(jnp.float32)
        dens_rows = lax.dynamic_slice_in_dim(res_density, start, RES, 0).astype(jnp.float32)
        pair_rows = pair_rows.reshape(RES, N_PW, pair_groups)
        dens_rows = dens_rows.reshape(RES, N_PW, screen_groups)
        results = []
        for step_index in range(1, STEPS + 1):
            other = ((block_index - step_index) % N_BLK) * VB
            other = other.astype(jnp.int32)
            vis_weight = lax.dynamic_slice_in_dim(weighted, other, VB, 0).astype(jnp.float32)
            vis_screen = lax.dynamic_slice_in_dim(screened, other, VB, 0).astype(jnp.float32)
            vis_weight = vis_weight.reshape(VB, N_PW, pair_groups)
            vis_screen = vis_screen.reshape(VB, N_PW, screen_groups)
            exchange_part = jnp.einsum("rpg,bpg->prb", pair_rows, vis_weight, precision=highest)
            direct_part = jnp.einsum("rpg,bpg->prb", dens_rows, vis_screen, precision=highest)
            partial_terms = 2.0 * exchange_part - direct_part
            results.append(jnp.sum(partial_terms, axis=0))
        return jnp.stack(results, axis=0)

    blocks = lax.map(one_block, jnp.arange(N_BLK, dtype=jnp.int32))
    return jnp.transpose(blocks, (1, 0, 2, 3)).reshape(STEPS, N_BLK * RES, VB)
```

```python
import functools

import jax
import jax.numpy as jnp
from jax import lax
from jax.experimental import pallas as pl
from jax.experimental.pallas import tpu as pltpu
from jax.sharding import PartitionSpec as P

NV = 200
NC = 300
N_X = 4
N_Z = 4
X_GROUPS = [[x * N_Z + z for x in range(N_X)] for z in range(N_Z)]
F32 = jnp.float32
BF16 = jnp.bfloat16
VMEM_LIMIT = 63 * 2**20
ANY = pl.BlockSpec(memory_space=pl.ANY)
SMEM = pl.BlockSpec(memory_space=pltpu.SMEM)
INDEX_ROWS = 16
OUTWARD = (2, 3)
INWARD = (1, 0)


def swapped_along_z(x, by):
    pairs = [(a * N_Z + z, a * N_Z + (z ^ by)) for a in range(N_X) for z in range(N_Z)]
    return lax.ppermute(x, "pw", pairs)


def call(kernel, name, out_shape, in_specs, scratch, flops):
    return pl.pallas_call(
        kernel,
        in_specs=in_specs,
        out_specs=jax.tree.map(lambda _: ANY, out_shape),
        out_shape=out_shape,
        scratch_shapes=scratch,
        compiler_params=pltpu.CompilerParams(vmem_limit_bytes=VMEM_LIMIT),
        cost_estimate=pl.CostEstimate(flops=flops, bytes_accessed=10**6, transcendentals=0),
        name=name,
    )


def picked_rows(form, rows):
    hits = lax.broadcasted_iota(jnp.int32, (rows.shape[0], form.shape[0]), 1) == rows
    return jnp.dot(hits.astype(F32).astype(BF16), form, preferred_element_type=F32)


def density(rows_val, rows_cond, val_form, cond_form):
    rows = jnp.concatenate([rows_val, rows_cond] * 4, axis=0).T
    picked = picked_rows(val_form, rows[:, 0:1]) * picked_rows(cond_form, rows[:, 1:2])
    return picked.astype(BF16)


def res_kernel(
    z_ref, pair_ref, val_ref, cond_ref, bands_ref, out_ref, in_ref, bands, val, cond, pair, dens, sems
):
    rows, groups = pair.shape
    own = rows // (N_X * N_Z)
    tables = table_copies((bands_ref, val_ref, cond_ref), (bands, val, cond), sems, 0)
    for copy in tables:
        copy.start()
    read = pltpu.make_async_copy(pair_ref, pair, sems.at[3])
    read.start()
    for copy in tables:
        copy.wait()
    rows_val = bands[2:3, :] * NV + bands[0:1, :]
    rows_cond = bands[2:3, :] * NC + bands[1:2, :]
    dens[...] = density(rows_val, rows_cond, val[...], cond[...])
    read.wait()
    gives = []
    for ref, steps in ((out_ref, OUTWARD), (in_ref, INWARD)):
        for x in range(N_X):
            for k, m in enumerate(steps):
                source = pl.ds(pl.multiple_of((x * N_Z + (z_ref[0] ^ m)) * own, own), own)
                target = ref.at[pl.ds((x * len(steps) + k) * own, own), :]
                at = 4 + 2 * len(gives) // 2
                gives.append(
                    pltpu.make_async_copy(
                        pair.at[source, :], target.at[:, pl.ds(0, groups)], sems.at[at]
                    )
                )
                gives.append(
                    pltpu.make_async_copy(
                        dens.at[source, :],
                        target.at[:, pl.ds(groups, dens.shape[1])],
                        sems.at[at + 1],
                    )
                )
    for give in gives:
        give.start()
    for give in gives:
        give.wait()


def table_copies(refs, places, sems, first):
    return [
        pltpu.make_async_copy(ref, place, sems.at[first + k])
        for k, (ref, place) in enumerate(zip(refs, places, strict=True))
    ]


def band_payload(band_pair, band_bands):
    rows_val = band_bands[2] * NV + band_bands[0]
    rows_cond = band_bands[2] * NC + band_bands[1]
    parts = jnp.stack([rows_val // 4, rows_val % 4, rows_cond // 4, rows_cond % 4])
    groups = band_pair.shape[1]
    parts = jnp.pad(parts, ((0, INDEX_ROWS - 4), (0, groups - parts.shape[1])))
    return jnp.concatenate([band_pair, parts.astype(BF16)], axis=0)


def product(left, right):
    return lax.dot_general(
        left, right, (((1,), (1,)), ((), ())), preferred_element_type=F32
    ).astype(BF16)


def out_kernel(
    odd_ref, left_ref, far_ref, even_ref, from_odd_ref, coulomb_ref, screening_ref, val_ref,
    cond_ref, out_ref, band_ref, near, far, coulomb, screening, val, cond, left, band, out, sems,
):
    cols, groups = near.shape[0] - INDEX_ROWS, near.shape[1]

    @pl.when(odd_ref[0] == 0)
    def _():
        pltpu.make_async_copy(from_odd_ref, near, sems.at[0]).start()

    @pl.when(odd_ref[0] != 0)
    def _():
        pltpu.make_async_copy(even_ref, near, sems.at[0]).start()

    refs = (far_ref, coulomb_ref, screening_ref, val_ref, cond_ref)
    copies = table_copies(refs, (far, coulomb, screening, val, cond), sems, 1)
    for copy in copies:
        copy.start()
    rows = pltpu.make_async_copy(left_ref, left, sems.at[6])
    rows.start()
    pltpu.make_async_copy(from_odd_ref, near, sems.at[0]).wait()
    for copy in copies:
        copy.wait()
    parts = jnp.concatenate([near[cols:, :cols], far[cols:, :cols]], axis=1)
    parts = parts.astype(F32).astype(jnp.int32)
    rows_val = parts[0:1, :] * 4 + parts[1:2, :]
    rows_cond = parts[2:3, :] * 4 + parts[3:4, :]
    dens = density(rows_val, rows_cond, val[...], cond[...])
    band[:, groups:] = -((dens.astype(F32) * screening[...]).astype(BF16))
    for k, payload in enumerate((near, far)):
        weighted = (payload[:cols, :].astype(F32) * coulomb[...]).astype(BF16)
        band[k * cols : (k + 1) * cols, :groups] = weighted * 2
    keep = pltpu.make_async_copy(band, band_ref, sems.at[0])
    keep.start()
    rows.wait()
    give_product(left, band, out, out_ref, sems)
    keep.wait()


def give_product(left, band, out, out_ref, sems, blocks=2):
    gives = []
    size = out.shape[0] // blocks
    for k in range(blocks):
        at = pl.ds(k * size, size)
        out[at, :] = product(left[at, :], band[...])
        gives.append(pltpu.make_async_copy(out.at[at, :], out_ref.at[at, :], sems.at[1 + k]))
        gives[-1].start()
    for give in gives:
        give.wait()


def in_kernel(left_ref, band_ref, out_ref, left, band, out, sems):
    rows = table_copies((left_ref, band_ref), (left, band), sems, 0)
    for copy in rows:
        copy.start()
    for copy in rows:
        copy.wait()
    give_product(left, band, out, out_ref, sems)


def shares_over_x(part):
    rows, cols = part.shape
    return lax.all_to_all(
        part.reshape(N_X, rows // N_X, cols), "pw", 0, 0, axis_index_groups=X_GROUPS
    )


def local(res_pair, band_pair, coulomb, screening, val_form, cond_form, res_bands, band_bands):
    rows, groups = res_pair.shape
    cols = band_pair.shape[0]
    depth = groups + val_form.shape[1]
    own = rows // (N_X * N_Z)
    half = rows // 2
    blocks = lax.axis_size("blk")
    payload = band_payload(band_pair, band_bands)
    far = lax.ppermute(payload, "blk", [(i, (i + 2) % blocks) for i in range(blocks)])
    from_even = lax.ppermute(payload, "blk", [(i, i + 1) for i in range(0, blocks, 2)])

    z = (lax.axis_index("pw") % N_Z).astype(jnp.int32)[None]
    odd = (lax.axis_index("blk") % 2).astype(jnp.int32)[None]
    tables = (coulomb[None, :], screening[None, :], val_form, cond_form)
    form_scratch = [pltpu.VMEM(t.shape, t.dtype) for t in tables]
    left = pltpu.VMEM((half, depth), BF16)
    band = pltpu.VMEM((2 * cols, depth), BF16)
    out = pltpu.VMEM((half, 2 * cols), BF16)
    block = pltpu.VMEM(payload.shape, BF16)
    left_shape = jax.ShapeDtypeStruct((half, depth), BF16)
    band_shape = jax.ShapeDtypeStruct((2 * cols, depth), BF16)
    term_shape = jax.ShapeDtypeStruct((half, 2 * cols), BF16)
    left_out, left_in = call(
        res_kernel,
        "res_rows",
        (left_shape, left_shape),
        [SMEM] + [ANY] * 4,
        [
            pltpu.VMEM(res_bands.shape, jnp.int32),
            *form_scratch[2:],
            pltpu.VMEM((rows, groups), BF16),
            pltpu.VMEM((rows, depth - groups), BF16),
            pltpu.SemaphoreType.DMA((4 + 4 * N_X * N_Z,)),
        ],
        2 * 10**9,
    )(z, res_pair, val_form, cond_form, res_bands)
    far, left_out, left_in, odd, tables = lax.optimization_barrier(
        (far, left_out, left_in, odd, tables)
    )
    from_odd = lax.ppermute(far, "blk", [(i + 1, i) for i in range(0, blocks, 2)])
    out_term, bands = call(
        out_kernel,
        "out_term",
        (term_shape, band_shape),
        [SMEM] + [ANY] * 8,
        [block, block, *form_scratch, left, band, out, pltpu.SemaphoreType.DMA((8,))],
        2 * 10**9,
    )(odd, left_out, far, from_even, from_odd, *tables)
    in_term = call(
        in_kernel,
        "in_term",
        term_shape,
        [ANY] * 2,
        [left, band, out, pltpu.SemaphoreType.DMA((4,))],
        2 * 10**9,
    )(left_in, bands)

    shares = shares_over_x(out_term)
    to_2 = jnp.sum(shares[:, :own].astype(F32), axis=0).astype(BF16)
    to_3 = jnp.sum(shares[:, own:].astype(F32), axis=0).astype(BF16)
    in_term, shares = lax.optimization_barrier((in_term, shares))
    from_2 = swapped_along_z(to_2, 2)
    from_3 = swapped_along_z(to_3, 3)
    shares = shares_over_x(in_term)
    to_1 = jnp.sum(shares[:, :own].astype(F32), axis=0).astype(BF16)
    from_1 = swapped_along_z(to_1, 1)
    total = jnp.sum(shares[:, own:].astype(F32), axis=0)
    total = total + from_2.astype(F32) + from_3.astype(F32) + from_1.astype(F32)
    return total.reshape(own, 2, cols).transpose(1, 0, 2)


def solution(mesh):
    return jax.shard_map(
        local,
        mesh=mesh,
        in_specs=(
            P("blk", "pw"),
            P("blk", "pw"),
            P("pw"),
            P("pw"),
            P(None, "pw"),
            P(None, "pw"),
            P(None, "blk"),
            P(None, "blk"),
        ),
        out_specs=P(None, ("blk", "pw"), None),
        check_vma=False,
    )
```

```python
import functools

import jax
import jax.numpy as jnp
from jax import lax
from jax.experimental import pallas as pl
from jax.experimental.pallas import tpu as pltpu
from jax.sharding import PartitionSpec as P

NV = 200
NC = 300
N_X = 4
N_Z = 4
X_GROUPS = [[x * N_Z + z for x in range(N_X)] for z in range(N_Z)]
F32 = jnp.float32
BF16 = jnp.bfloat16
VMEM_LIMIT = 63 * 2**20
ANY = pl.BlockSpec(memory_space=pl.ANY)
INDEX_ROWS = 16
FIRST_ROWS = (2, 0)
OTHER_ROWS = (1, 3)


def along_z(x, by):
    pairs = [(a * N_Z + z, a * N_Z + (z + by) % N_Z) for a in range(N_X) for z in range(N_Z)]
    return lax.ppermute(x, "pw", pairs)


def call(kernel, name, out_shape, in_specs, scratch, flops):
    return pl.pallas_call(
        kernel,
        in_specs=in_specs,
        out_specs=jax.tree.map(lambda _: ANY, out_shape),
        out_shape=out_shape,
        scratch_shapes=scratch,
        compiler_params=pltpu.CompilerParams(vmem_limit_bytes=VMEM_LIMIT),
        cost_estimate=pl.CostEstimate(flops=flops, bytes_accessed=10**6, transcendentals=0),
        name=name,
    )


def picked_rows(form, rows):
    hits = lax.broadcasted_iota(jnp.int32, (rows.shape[0], form.shape[0]), 1) == rows
    return jnp.dot(hits.astype(F32).astype(BF16), form, preferred_element_type=F32)


def density(rows_val, rows_cond, val_form, cond_form):
    rows = jnp.concatenate([rows_val, rows_cond] * 4, axis=0).T
    picked = picked_rows(val_form, rows[:, 0:1]) * picked_rows(cond_form, rows[:, 1:2])
    return picked.astype(BF16)


def res_kernel(
    pair_ref, val_ref, cond_ref, bands_ref, out_ref, in_ref, bands, val, cond, pair, dens, sems
):
    rows, groups = pair.shape
    own = rows // (N_X * N_Z)
    pw = lax.axis_index("pw")
    my_x, my_z = pw // N_Z, pw % N_Z
    tables = table_copies((bands_ref, val_ref, cond_ref), (bands, val, cond), sems, 0)
    for copy in tables:
        copy.start()
    reads = split_copies(pair_ref, pair, sems, 4, 4)
    for read in reads:
        read.start()
    for copy in tables:
        copy.wait()
    rows_val = bands[2:3, :] * NV + bands[0:1, :]
    rows_cond = bands[2:3, :] * NC + bands[1:2, :]
    dens[...] = density(rows_val, rows_cond, val[...], cond[...])
    for read in reads:
        read.wait()
    gives = []
    for ref, steps in ((out_ref, FIRST_ROWS), (in_ref, OTHER_ROWS)):
        for x in range(N_X):
            for k, m in enumerate(steps):
                owner_x = x if ref is out_ref else (x + my_x) % N_X
                owner = owner_x * N_Z + (my_z + m) % N_Z
                source = pl.ds(pl.multiple_of(owner * own, own), own)
                target = ref.at[pl.ds((x * len(steps) + k) * own, own), :]
                at = 4 + 2 * len(gives) // 2
                gives.append(
                    pltpu.make_async_copy(
                        pair.at[source, :], target.at[:, pl.ds(0, groups)], sems.at[at]
                    )
                )
                gives.append(
                    pltpu.make_async_copy(
                        dens.at[source, :],
                        target.at[:, pl.ds(groups, dens.shape[1])],
                        sems.at[at + 1],
                    )
                )
    for give in gives:
        give.start()
    for give in gives:
        give.wait()


def split_copies(source, target, sems, first, count):
    size = source.shape[0] // count
    return [
        pltpu.make_async_copy(
            source.at[pl.ds(k * size, size), :], target.at[pl.ds(k * size, size), :], sems.at[first + k]
        )
        for k in range(count)
    ]


def table_copies(refs, places, sems, first):
    return [
        pltpu.make_async_copy(ref, place, sems.at[first + k])
        for k, (ref, place) in enumerate(zip(refs, places, strict=True))
    ]


def payload_kernel(pair_ref, bands_ref, out_ref, bands, sems):
    cols, groups = pair_ref.shape
    read = pltpu.make_async_copy(bands_ref, bands, sems.at[0])
    read.start()
    moves = split_copies(pair_ref, out_ref.at[pl.ds(0, cols), :], sems, 1, 4)
    for move in moves:
        move.start()
    read.wait()
    rows_val = bands[2:3, :] * NV + bands[0:1, :]
    rows_cond = bands[2:3, :] * NC + bands[1:2, :]
    codes = [rows_val // 4, rows_val % 4, rows_cond // 4, rows_cond % 4]
    codes = jnp.concatenate(codes * (INDEX_ROWS // 4), axis=0)
    codes = jnp.concatenate([codes] * (groups // cols), axis=1)
    out_ref[cols:, :] = codes.astype(F32).astype(BF16)
    for move in moves:
        move.wait()


def band_payload(band_pair, band_bands):
    cols, groups = band_pair.shape
    return pl.pallas_call(
        payload_kernel,
        in_specs=[ANY] * 2,
        out_specs=pl.BlockSpec(memory_space=pltpu.VMEM),
        out_shape=jax.ShapeDtypeStruct((cols + INDEX_ROWS, groups), BF16),
        scratch_shapes=[
            pltpu.VMEM(band_bands.shape, jnp.int32),
            pltpu.SemaphoreType.DMA((5,)),
        ],
        compiler_params=pltpu.CompilerParams(vmem_limit_bytes=60 * 2**20),
        cost_estimate=pl.CostEstimate(flops=10**7, bytes_accessed=10**6, transcendentals=0),
        name="band_payload",
    )(band_pair, band_bands)


def product(left, right):
    return lax.dot_general(
        left, right, (((1,), (1,)), ((), ())), preferred_element_type=F32
    ).astype(BF16)


def out_kernel(
    left_ref, far_ref, even_ref, from_odd_ref, coulomb_ref, screening_ref, val_ref,
    cond_ref, out_ref, band_ref, near, far, coulomb, screening, val, cond, left, band, out, sems,
):
    cols, groups = near.shape[0] - INDEX_ROWS, near.shape[1]

    odd = lax.axis_index("blk") % 2

    @pl.when(odd == 0)
    def _():
        pltpu.make_async_copy(from_odd_ref, near, sems.at[0]).start()

    @pl.when(odd != 0)
    def _():
        pltpu.make_async_copy(even_ref, near, sems.at[0]).start()

    refs = (far_ref, coulomb_ref, screening_ref, val_ref, cond_ref)
    copies = table_copies(refs, (far, coulomb, screening, val, cond), sems, 1)
    for copy in copies:
        copy.start()
    rows = split_copies(left_ref, left, sems, 6, 4)
    for row in rows:
        row.start()
    pltpu.make_async_copy(from_odd_ref, near, sems.at[0]).wait()
    for copy in copies:
        copy.wait()
    parts = jnp.concatenate([near[cols:, :cols], far[cols:, :cols]], axis=1)
    parts = parts.astype(F32).astype(jnp.int32)
    rows_val = parts[0:1, :] * 4 + parts[1:2, :]
    rows_cond = parts[2:3, :] * 4 + parts[3:4, :]
    dens = density(rows_val, rows_cond, val[...], cond[...])
    band[:, groups:] = -((dens.astype(F32) * screening[...][None, :]).astype(BF16))
    for k, payload in enumerate((near, far)):
        weighted = (payload[:cols, :].astype(F32) * coulomb[...][None, :]).astype(BF16)
        band[k * cols : (k + 1) * cols, :groups] = weighted * 2
    keep = pltpu.make_async_copy(band, band_ref, sems.at[0])
    keep.start()
    for row in rows:
        row.wait()
    half = out.shape[0] // 2
    halves = (out_ref.at[pl.ds(0, half)], out_ref.at[pl.ds(half, half)])
    give_product(left, band, out, halves, sems)
    keep.wait()


def give_product(left, band, out, out_refs, sems):
    gives = []
    count, steps, own, cols = out.shape
    each = count // len(out_refs)
    for k, ref in enumerate(out_refs):
        total = product(left[pl.ds(k * each * own, each * own), :], band[...])
        for n in range(each):
            for step in range(steps):
                out[k * each + n, step] = total[
                    n * own : (n + 1) * own, step * cols : (step + 1) * cols
                ]
        gives.append(pltpu.make_async_copy(out.at[pl.ds(k * each, each)], ref, sems.at[1 + k]))
        gives[-1].start()
    for give in gives:
        give.wait()


def in_kernel(left_ref, band_ref, out_0, out_1, out_2, out_3, left, band, out, sems):
    rows = split_copies(left_ref, left, sems, 5, 4) + split_copies(band_ref, band, sems, 9, 2)
    for copy in rows:
        copy.start()
    for copy in rows:
        copy.wait()
    give_product(left, band, out, (out_0, out_1, out_2, out_3), sems)


def along_x(x, by):
    pairs = [(a * N_Z + z, (a + by) % N_X * N_Z + z) for a in range(N_X) for z in range(N_Z)]
    return lax.ppermute(x, "pw", pairs)


def shares_over_x(pieces):
    return lax.all_to_all(pieces, "pw", 0, 0, axis_index_groups=X_GROUPS, tiled=True)


def local(res_pair, band_pair, coulomb, screening, val_form, cond_form, res_bands, band_bands):
    rows, groups = res_pair.shape
    cols = band_pair.shape[0]
    depth = groups + val_form.shape[1]
    own = rows // (N_X * N_Z)
    few, many = (rows * len(steps) // N_Z for steps in (FIRST_ROWS, OTHER_ROWS))
    blocks = lax.axis_size("blk")
    payload = band_payload(band_pair, band_bands)
    far = lax.ppermute(payload, "blk", [(i, (i + 2) % blocks) for i in range(blocks)])
    from_even = lax.ppermute(payload, "blk", [(i, i + 1) for i in range(0, blocks, 2)])

    tables = (coulomb, screening, val_form, cond_form)
    form_scratch = [pltpu.VMEM(t.shape, t.dtype) for t in tables]
    band = pltpu.VMEM((2 * cols, depth), BF16)
    block = pltpu.VMEM(payload.shape, BF16)
    band_shape = jax.ShapeDtypeStruct((2 * cols, depth), BF16)
    left_out, left_in = call(
        res_kernel,
        "res_rows",
        tuple(jax.ShapeDtypeStruct((n, depth), BF16) for n in (few, many)),
        [ANY] * 4,
        [
            pltpu.VMEM(res_bands.shape, jnp.int32),
            *form_scratch[2:],
            pltpu.VMEM((rows, groups), BF16),
            pltpu.VMEM((rows, depth - groups), BF16),
            pltpu.SemaphoreType.DMA((4 + 4 * N_X * N_Z,)),
        ],
        2 * 10**9,
    )(res_pair, val_form, cond_form, res_bands)
    far, left_out, left_in, tables = lax.optimization_barrier((far, left_out, left_in, tables))
    from_odd = lax.ppermute(far, "blk", [(i + 1, i) for i in range(0, blocks, 2)])
    out_term, bands = call(
        out_kernel,
        "out_term",
        (jax.ShapeDtypeStruct((few // own, 2, own, cols), BF16), band_shape),
        [ANY] * 8,
        [
            block,
            block,
            *form_scratch,
            pltpu.VMEM((few, depth), BF16),
            band,
            pltpu.VMEM((few // own, 2, own, cols), BF16),
            pltpu.SemaphoreType.DMA((10,)),
        ],
        2 * 10**9,
    )(left_out, far, from_even, from_odd, *tables)
    in_terms = call(
        in_kernel,
        "in_term",
        (jax.ShapeDtypeStruct((len(OTHER_ROWS), 2, own, cols), BF16),) * N_X,
        [ANY] * 2,
        [
            pltpu.VMEM((many, depth), BF16),
            band,
            pltpu.VMEM((many // own, 2, own, cols), BF16),
            pltpu.SemaphoreType.DMA((11,)),
        ],
        2 * 10**9,
    )(left_in, bands)

    first_shares = shares_over_x(out_term)
    to_2 = jnp.sum(first_shares[0::2].astype(F32), axis=0).astype(BF16)
    from_2 = along_z(to_2, 2)
    own_share, _ = lax.optimization_barrier((in_terms[0], to_2))
    shares = [own_share] + [along_x(in_terms[by], by) for by in (1, 3, 2)]

    def summed(k):
        return sum(s[k].astype(F32) for s in shares)

    to_1, to_3 = summed(0).astype(BF16), summed(1).astype(BF16)
    from_1 = along_z(to_1, 1)
    from_3 = along_z(to_3, 3)
    first_shares, _, _ = lax.optimization_barrier((first_shares, to_1, to_3))
    total = jnp.sum(first_shares[1::2].astype(F32), axis=0)
    total, from_2 = lax.optimization_barrier((total, from_2))
    return total + from_2.astype(F32) + from_1.astype(F32) + from_3.astype(F32)


def solution(mesh):
    return jax.shard_map(
        local,
        mesh=mesh,
        in_specs=(
            P("blk", "pw"),
            P("blk", "pw"),
            P("pw"),
            P("pw"),
            P(None, "pw"),
            P(None, "pw"),
            P(None, "blk"),
            P(None, "blk"),
        ),
        out_specs=P(None, ("blk", "pw"), None),
        check_vma=False,
    )
```

```python
import functools

import jax
import jax.numpy as jnp
from jax import lax
from jax.experimental import pallas as pl
from jax.experimental.pallas import tpu as pltpu
from jax.sharding import PartitionSpec as P

NV = 200
NC = 300
N_X = 4
N_Z = 4
X_GROUPS = [[x * N_Z + z for x in range(N_X)] for z in range(N_Z)]
F32 = jnp.float32
BF16 = jnp.bfloat16
VMEM_LIMIT = 63 * 2**20
ANY = pl.BlockSpec(memory_space=pl.ANY)
VMEM = pl.BlockSpec(memory_space=pltpu.VMEM)
FIRST_ROWS = (2,)
OTHER_ROWS = (1, 3, 0)


def along_z(x, by):
    pairs = [(a * N_Z + z, a * N_Z + (z + by) % N_Z) for a in range(N_X) for z in range(N_Z)]
    return lax.ppermute(x, "pw", pairs)


def call(kernel, name, out_shape, in_specs, scratch, flops):
    return pl.pallas_call(
        kernel,
        in_specs=in_specs,
        out_specs=jax.tree.map(lambda _: ANY, out_shape),
        out_shape=out_shape,
        scratch_shapes=scratch,
        compiler_params=pltpu.CompilerParams(vmem_limit_bytes=VMEM_LIMIT),
        cost_estimate=pl.CostEstimate(flops=flops, bytes_accessed=10**6, transcendentals=0),
        name=name,
    )


def picked_rows(form, rows):
    hits = lax.broadcasted_iota(jnp.int32, (rows.shape[0], form.shape[0]), 1) == rows
    return jnp.dot(hits.astype(F32).astype(BF16), form, preferred_element_type=F32)


def density(rows_val, rows_cond, val_form, cond_form):
    rows = jnp.concatenate([rows_val, rows_cond] * 4, axis=0).T
    picked = picked_rows(val_form, rows[:, 0:1]) * picked_rows(cond_form, rows[:, 1:2])
    return picked.astype(BF16)


def res_kernel(
    pair_ref, val_ref, cond_ref, bands_ref, out_ref, in_ref, bands, val, cond, pair, dens, sems
):
    rows, groups = pair.shape
    own = rows // (N_X * N_Z)
    pw = lax.axis_index("pw")
    my_x, my_z = pw // N_Z, pw % N_Z
    tables = table_copies((bands_ref, val_ref, cond_ref), (bands, val, cond), sems, 0)
    for copy in tables:
        copy.start()
    read = pltpu.make_async_copy(pair_ref, pair, sems.at[3])
    read.start()
    for copy in tables:
        copy.wait()
    rows_val = bands[2:3, :] * NV + bands[0:1, :]
    rows_cond = bands[2:3, :] * NC + bands[1:2, :]
    dens[...] = density(rows_val, rows_cond, val[...], cond[...])
    read.wait()
    gives = []
    for ref, steps in ((out_ref, FIRST_ROWS), (in_ref, OTHER_ROWS)):
        for x in range(N_X):
            for k, m in enumerate(steps):
                owner_x = x if ref is out_ref else (x + my_x) % N_X
                owner = owner_x * N_Z + (my_z + m) % N_Z
                source = pl.ds(pl.multiple_of(owner * own, own), own)
                target = ref.at[pl.ds((x * len(steps) + k) * own, own), :]
                at = 4 + 2 * len(gives) // 2
                gives.append(
                    pltpu.make_async_copy(
                        pair.at[source, :], target.at[:, pl.ds(0, groups)], sems.at[at]
                    )
                )
                gives.append(
                    pltpu.make_async_copy(
                        dens.at[source, :],
                        target.at[:, pl.ds(groups, dens.shape[1])],
                        sems.at[at + 1],
                    )
                )
    for give in gives:
        give.start()
    for give in gives:
        give.wait()


def table_copies(refs, places, sems, first):
    return [
        pltpu.make_async_copy(ref, place, sems.at[first + k])
        for k, (ref, place) in enumerate(zip(refs, places, strict=True))
    ]


def product(left, right):
    return lax.dot_general(
        left, right, (((1,), (1,)), ((), ())), preferred_element_type=F32
    ).astype(BF16)


def out_kernel(
    left_ref, far_ref, even_ref, from_odd_ref, far_bands_ref, near_bands_ref,
    coulomb_ref, screening_ref, val_ref, cond_ref, out_ref, band_ref, near, far, near_bands,
    far_bands, coulomb, screening, val, cond, left, band, out, sems,
):
    cols, groups = near.shape

    odd = lax.axis_index("blk") % 2

    @pl.when(odd == 0)
    def _():
        pltpu.make_async_copy(from_odd_ref, near, sems.at[0]).start()

    @pl.when(odd != 0)
    def _():
        pltpu.make_async_copy(even_ref, near, sems.at[0]).start()

    refs = (far_ref, coulomb_ref, screening_ref, val_ref, cond_ref)
    copies = table_copies(refs, (far, coulomb, screening, val, cond), sems, 1)
    copies += table_copies((near_bands_ref, far_bands_ref), (near_bands, far_bands), sems, 10)
    for copy in copies:
        copy.start()
    rows = pltpu.make_async_copy(left_ref, left, sems.at[6])
    rows.start()
    pltpu.make_async_copy(from_odd_ref, near, sems.at[0]).wait()
    for copy in copies:
        copy.wait()
    bands = jnp.concatenate([near_bands[...], far_bands[...]], axis=1)
    rows_val = bands[2:3, :] * NV + bands[0:1, :]
    rows_cond = bands[2:3, :] * NC + bands[1:2, :]
    dens = density(rows_val, rows_cond, val[...], cond[...])
    band[:, groups:] = -((dens.astype(F32) * screening[...][None, :]).astype(BF16))
    for k, payload in enumerate((near, far)):
        weighted = (payload[...].astype(F32) * coulomb[...][None, :]).astype(BF16)
        band[k * cols : (k + 1) * cols, :groups] = weighted * 2
    keep = pltpu.make_async_copy(band, band_ref, sems.at[0])
    keep.start()
    rows.wait()
    half = out.shape[0] // 2
    halves = (out_ref.at[pl.ds(0, half)], out_ref.at[pl.ds(half, half)])
    give_product(left, band, out, halves, sems)
    keep.wait()


def give_product(left, band, out, out_refs, sems):
    gives = []
    count, steps, own, cols = out.shape
    each = count // len(out_refs)
    for k, ref in enumerate(out_refs):
        total = product(left[pl.ds(k * each * own, each * own), :], band[...])
        for n in range(each):
            for step in range(steps):
                out[k * each + n, step] = total[
                    n * own : (n + 1) * own, step * cols : (step + 1) * cols
                ]
        gives.append(pltpu.make_async_copy(out.at[pl.ds(k * each, each)], ref, sems.at[1 + k]))
        gives[-1].start()
    for give in gives:
        give.wait()


def in_kernel(
    left_ref, band_ref, out_0, out_1, out_2, out_3, own_ref, left, band, out, sems, out_sems
):
    rows = table_copies((left_ref, band_ref), (left, band), sems, 0)
    for copy in rows:
        copy.start()
    for copy in rows:
        copy.wait()
    my_x = lax.axis_index("pw") // N_Z
    count, steps, own, cols = out.shape
    each = count // N_X
    gives = []
    for by, ref in ((1, out_1), (3, out_3), (2, out_2), (0, out_0)):
        total = product(left[pl.ds(by * each * own, each * own), :], band[...])
        for n in range(each):
            for step in range(steps):
                out[by * each + n, step] = total[
                    n * own : (n + 1) * own, step * cols : (step + 1) * cols
                ]
        owner = own_ref.at[pl.ds((my_x + by) % N_X, 1)]
        gives += [
            pltpu.make_async_copy(
                out.at[pl.ds(by * each, each - 1)], ref, out_sems.at[2 * by]
            ),
            pltpu.make_async_copy(
                out.at[pl.ds(by * each + each - 1, 1)], owner, out_sems.at[2 * by + 1]
            ),
        ]
        gives[-2].start()
        gives[-1].start()
    for give in gives:
        give.wait()


def along_x(x, by):
    pairs = [(a * N_Z + z, (a + by) % N_X * N_Z + z) for a in range(N_X) for z in range(N_Z)]
    return lax.ppermute(x, "pw", pairs)


def taken_kernel(first_ref, second_ref, third_ref, out_ref):
    out_ref[...] = (
        first_ref[...].astype(F32) + second_ref[...].astype(F32) + third_ref[...].astype(F32)
    )


def shares_over_x(pieces):
    return lax.all_to_all(pieces, "pw", 0, 0, axis_index_groups=X_GROUPS)


def local(res_pair, band_pair, coulomb, screening, val_form, cond_form, res_bands, band_bands):
    rows, groups = res_pair.shape
    cols = band_pair.shape[0]
    depth = groups + val_form.shape[1]
    own = rows // (N_X * N_Z)
    few, many = (rows * len(steps) // N_Z for steps in (FIRST_ROWS, OTHER_ROWS))
    blocks = lax.axis_size("blk")
    far_on = [(i, (i + 2) % blocks) for i in range(blocks)]
    far = lax.ppermute(band_pair, "blk", far_on)
    far_bands = lax.ppermute(band_bands, "blk", far_on)
    near_bands = lax.ppermute(band_bands, "blk", [(i, (i + 1) % blocks) for i in range(blocks)])
    from_even = lax.ppermute(band_pair, "blk", [(i, i + 1) for i in range(0, blocks, 2)])

    tables = (coulomb, screening, val_form, cond_form)
    form_scratch = [pltpu.VMEM(t.shape, t.dtype) for t in tables]
    band = pltpu.VMEM((2 * cols, depth), BF16)
    block = pltpu.VMEM(band_pair.shape, BF16)
    index = pltpu.VMEM(band_bands.shape, jnp.int32)
    band_shape = jax.ShapeDtypeStruct((2 * cols, depth), BF16)
    left_out, left_in = call(
        res_kernel,
        "res_rows",
        tuple(jax.ShapeDtypeStruct((n, depth), BF16) for n in (few, many)),
        [ANY] * 4,
        [
            pltpu.VMEM(res_bands.shape, jnp.int32),
            *form_scratch[2:],
            pltpu.VMEM((rows, groups), BF16),
            pltpu.VMEM((rows, depth - groups), BF16),
            pltpu.SemaphoreType.DMA((4 + 4 * N_X * N_Z,)),
        ],
        2 * 10**9,
    )(res_pair, val_form, cond_form, res_bands)
    far, far_bands, near_bands, left_out, left_in, tables = lax.optimization_barrier(
        (far, far_bands, near_bands, left_out, left_in, tables)
    )
    from_odd = lax.ppermute(far, "blk", [(i + 1, i) for i in range(0, blocks, 2)])
    out_term, bands = call(
        out_kernel,
        "out_term",
        (jax.ShapeDtypeStruct((few // own, 2, own, cols), BF16), band_shape),
        [ANY] * 10,
        [
            block,
            block,
            index,
            index,
            *form_scratch,
            pltpu.VMEM((few, depth), BF16),
            band,
            pltpu.VMEM((few // own, 2, own, cols), BF16),
            pltpu.SemaphoreType.DMA((12,)),
        ],
        2 * 10**9,
    )(left_out, far, from_even, from_odd, far_bands, near_bands, *tables)
    *in_terms, own_terms = call(
        in_kernel,
        "in_term",
        (jax.ShapeDtypeStruct((len(OTHER_ROWS) - 1, 2, own, cols), BF16),) * N_X
        + (jax.ShapeDtypeStruct((N_X, 2, own, cols), BF16),),
        [ANY] * 2,
        [
            pltpu.VMEM((many, depth), BF16),
            band,
            pltpu.VMEM((many // own, 2, own, cols), BF16),
            pltpu.SemaphoreType.DMA((2,)),
            pltpu.SemaphoreType.DMA((2 * N_X,)),
        ],
        2 * 10**9,
    )(left_in, bands)

    to_2 = jnp.sum(shares_over_x(out_term).astype(F32), axis=0).astype(BF16)
    from_2 = along_z(to_2, 2)
    own_share, _ = lax.optimization_barrier((in_terms[0], to_2))
    shares = [own_share] + [along_x(in_terms[by], by) for by in (1, 3, 2)]

    def summed(k):
        return sum(s[k].astype(F32) for s in shares)

    to_1, to_3 = summed(0).astype(BF16), summed(1).astype(BF16)
    from_1 = along_z(to_1, 1)
    from_3 = along_z(to_3, 3)
    own_terms, _, _ = lax.optimization_barrier((own_terms, to_1, to_3))
    total = jnp.sum(shares_over_x(own_terms).astype(F32), axis=0)
    taken = pl.pallas_call(
        taken_kernel,
        in_specs=[VMEM] * 3,
        out_specs=VMEM,
        out_shape=jax.ShapeDtypeStruct(from_2.shape, F32),
        compiler_params=pltpu.CompilerParams(vmem_limit_bytes=4 * 2**20),
        cost_estimate=pl.CostEstimate(flops=8000000000, bytes_accessed=10**6, transcendentals=0),
        name="taken",
    )(from_2, from_3, from_1)
    return total + taken


def solution(mesh):
    return jax.shard_map(
        local,
        mesh=mesh,
        in_specs=(
            P("blk", "pw"),
            P("blk", "pw"),
            P("pw"),
            P("pw"),
            P(None, "pw"),
            P(None, "pw"),
            P(None, "blk"),
            P(None, "blk"),
        ),
        out_specs=P(None, ("blk", "pw"), None),
        check_vma=False,
    )
```

```python
import functools

import jax
import jax.numpy as jnp
from jax import lax
from jax.experimental import pallas as pl
from jax.experimental.pallas import tpu as pltpu
from jax.sharding import PartitionSpec as P

NV = 200
NC = 300
N_X = 4
N_Z = 4
X_GROUPS = [[x * N_Z + z for x in range(N_X)] for z in range(N_Z)]
F32 = jnp.float32
BF16 = jnp.bfloat16
VMEM_LIMIT = 63 * 2**20
ANY = pl.BlockSpec(memory_space=pl.ANY)
VMEM = pl.BlockSpec(memory_space=pltpu.VMEM)
FIRST_ROWS = (2,)
OTHER_ROWS = (1, 3, 0)


def along_z(x, by):
    pairs = [(a * N_Z + z, a * N_Z + (z + by) % N_Z) for a in range(N_X) for z in range(N_Z)]
    return lax.ppermute(x, "pw", pairs)


def call(kernel, name, out_shape, in_specs, scratch, flops):
    return pl.pallas_call(
        kernel,
        in_specs=in_specs,
        out_specs=jax.tree.map(lambda _: ANY, out_shape),
        out_shape=out_shape,
        scratch_shapes=scratch,
        compiler_params=pltpu.CompilerParams(vmem_limit_bytes=VMEM_LIMIT),
        cost_estimate=pl.CostEstimate(flops=flops, bytes_accessed=10**6, transcendentals=0),
        name=name,
    )


def picked_rows(form, rows):
    hits = lax.broadcasted_iota(jnp.int32, (rows.shape[0], form.shape[0]), 1) == rows
    return jnp.dot(hits.astype(F32).astype(BF16), form, preferred_element_type=F32)


def density(rows_val, rows_cond, val_form, cond_form):
    rows = jnp.concatenate([rows_val, rows_cond] * 4, axis=0).T
    picked = picked_rows(val_form, rows[:, 0:1]) * picked_rows(cond_form, rows[:, 1:2])
    return picked.astype(BF16)


def res_kernel(
    pair_ref, val_ref, cond_ref, bands_ref, out_ref, in_ref, bands, val, cond, pair, dens, sems
):
    rows, groups = pair.shape
    own = rows // (N_X * N_Z)
    pw = lax.axis_index("pw")
    my_x, my_z = pw // N_Z, pw % N_Z
    tables = table_copies((bands_ref, val_ref, cond_ref), (bands, val, cond), sems, 0)
    for copy in tables:
        copy.start()
    read = pltpu.make_async_copy(pair_ref, pair, sems.at[3])
    read.start()
    for copy in tables:
        copy.wait()
    rows_val = bands[2:3, :] * NV + bands[0:1, :]
    rows_cond = bands[2:3, :] * NC + bands[1:2, :]
    half = rows // 2
    dens[:half, :] = density(rows_val[:, :half], rows_cond[:, :half], val[...], cond[...])
    read.wait()
    gives = []
    later = []
    for ref, steps in ((out_ref, FIRST_ROWS), (in_ref, OTHER_ROWS)):
        for x in range(N_X):
            for k, m in enumerate(steps):
                owner_x = x if ref is out_ref else (x + my_x) % N_X
                owner = owner_x * N_Z + (my_z + m) % N_Z
                source = pl.ds(pl.multiple_of(owner * own, own), own)
                target = ref.at[pl.ds((x * len(steps) + k) * own, own), :]
                at = 4 + 2 * len(gives)
                gives.append(
                    pltpu.make_async_copy(
                        pair.at[source, :], target.at[:, pl.ds(0, groups)], sems.at[at]
                    )
                )
                gives[-1].start()
                later.append(
                    pltpu.make_async_copy(
                        dens.at[source, :],
                        target.at[:, pl.ds(groups, dens.shape[1])],
                        sems.at[at + 1],
                    )
                )
    dens[half:, :] = density(rows_val[:, half:], rows_cond[:, half:], val[...], cond[...])
    for give in later:
        give.start()
    for give in gives + later:
        give.wait()


def table_copies(refs, places, sems, first):
    return [
        pltpu.make_async_copy(ref, place, sems.at[first + k])
        for k, (ref, place) in enumerate(zip(refs, places, strict=True))
    ]


def product(left, right):
    return lax.dot_general(
        left, right, (((1,), (1,)), ((), ())), preferred_element_type=F32
    ).astype(BF16)


def out_kernel(
    left_ref, far_ref, even_ref, from_odd_ref, far_bands_ref, near_bands_ref,
    coulomb_ref, screening_ref, val_ref, cond_ref, out_ref, band_ref, near, far, near_bands,
    far_bands, coulomb, screening, val, cond, left, band, out, sems,
):
    cols, groups = near.shape

    odd = lax.axis_index("blk") % 2

    @pl.when(odd == 0)
    def _():
        pltpu.make_async_copy(from_odd_ref, near, sems.at[0]).start()

    @pl.when(odd != 0)
    def _():
        pltpu.make_async_copy(even_ref, near, sems.at[0]).start()

    refs = (far_ref, coulomb_ref, screening_ref, val_ref, cond_ref)
    copies = table_copies(refs, (far, coulomb, screening, val, cond), sems, 1)
    copies += table_copies((near_bands_ref, far_bands_ref), (near_bands, far_bands), sems, 10)
    for copy in copies:
        copy.start()
    rows = pltpu.make_async_copy(left_ref, left, sems.at[6])
    rows.start()
    pltpu.make_async_copy(from_odd_ref, near, sems.at[0]).wait()
    for copy in copies:
        copy.wait()
    bands = jnp.concatenate([near_bands[...], far_bands[...]], axis=1)
    rows_val = bands[2:3, :] * NV + bands[0:1, :]
    rows_cond = bands[2:3, :] * NC + bands[1:2, :]
    dens = density(rows_val, rows_cond, val[...], cond[...])
    band[:, groups:] = -((dens.astype(F32) * screening[...][None, :]).astype(BF16))
    for k, payload in enumerate((near, far)):
        weighted = (payload[...].astype(F32) * coulomb[...][None, :]).astype(BF16)
        band[k * cols : (k + 1) * cols, :groups] = weighted * 2
    keep = pltpu.make_async_copy(band, band_ref, sems.at[0])
    keep.start()
    rows.wait()
    half = out.shape[0] // 2
    halves = (out_ref.at[pl.ds(0, half)], out_ref.at[pl.ds(half, half)])
    give_product(left, band, out, halves, sems)
    keep.wait()


def give_product(left, band, out, out_refs, sems):
    gives = []
    count, steps, own, cols = out.shape
    each = count // len(out_refs)
    for k, ref in enumerate(out_refs):
        total = product(left[pl.ds(k * each * own, each * own), :], band[...])
        for n in range(each):
            for step in range(steps):
                out[k * each + n, step] = total[
                    n * own : (n + 1) * own, step * cols : (step + 1) * cols
                ]
        gives.append(pltpu.make_async_copy(out.at[pl.ds(k * each, each)], ref, sems.at[1 + k]))
        gives[-1].start()
    for give in gives:
        give.wait()


def in_kernel(
    left_ref, band_ref, out_0, out_1, out_2, out_3, own_ref, left, band, out, sems, out_sems
):
    rows = table_copies((left_ref, band_ref), (left, band), sems, 0)
    for copy in rows:
        copy.start()
    for copy in rows:
        copy.wait()
    my_x = lax.axis_index("pw") // N_Z
    count, steps, own, cols = out.shape
    each = count // N_X
    gives = []
    for by, ref in ((1, out_1), (3, out_3), (2, out_2), (0, out_0)):
        total = product(left[pl.ds(by * each * own, each * own), :], band[...])
        for n in range(each):
            for step in range(steps):
                out[by * each + n, step] = total[
                    n * own : (n + 1) * own, step * cols : (step + 1) * cols
                ]
        owner = own_ref.at[pl.ds((my_x + by) % N_X, 1)]
        gives += [
            pltpu.make_async_copy(
                out.at[pl.ds(by * each, each - 1)], ref, out_sems.at[2 * by]
            ),
            pltpu.make_async_copy(
                out.at[pl.ds(by * each + each - 1, 1)], owner, out_sems.at[2 * by + 1]
            ),
        ]
        gives[-2].start()
        gives[-1].start()
    for give in gives:
        give.wait()


def along_x(x, by):
    pairs = [(a * N_Z + z, (a + by) % N_X * N_Z + z) for a in range(N_X) for z in range(N_Z)]
    return lax.ppermute(x, "pw", pairs)


def taken_kernel(first_ref, second_ref, third_ref, out_ref):
    out_ref[...] = (
        first_ref[...].astype(F32) + second_ref[...].astype(F32) + third_ref[...].astype(F32)
    )


def shares_over_x(pieces):
    return lax.all_to_all(pieces, "pw", 0, 0, axis_index_groups=X_GROUPS)


def local(res_pair, band_pair, coulomb, screening, val_form, cond_form, res_bands, band_bands):
    rows, groups = res_pair.shape
    cols = band_pair.shape[0]
    depth = groups + val_form.shape[1]
    own = rows // (N_X * N_Z)
    few, many = (rows * len(steps) // N_Z for steps in (FIRST_ROWS, OTHER_ROWS))
    blocks = lax.axis_size("blk")
    far_on = [(i, (i + 2) % blocks) for i in range(blocks)]
    far = lax.ppermute(band_pair, "blk", far_on)
    far_bands = lax.ppermute(band_bands, "blk", far_on)
    near_bands = lax.ppermute(band_bands, "blk", [(i, (i + 1) % blocks) for i in range(blocks)])
    from_even = lax.ppermute(band_pair, "blk", [(i, i + 1) for i in range(0, blocks, 2)])

    tables = (coulomb, screening, val_form, cond_form)
    form_scratch = [pltpu.VMEM(t.shape, t.dtype) for t in tables]
    band = pltpu.VMEM((2 * cols, depth), BF16)
    block = pltpu.VMEM(band_pair.shape, BF16)
    index = pltpu.VMEM(band_bands.shape, jnp.int32)
    band_shape = jax.ShapeDtypeStruct((2 * cols, depth), BF16)
    left_out, left_in = call(
        res_kernel,
        "res_rows",
        tuple(jax.ShapeDtypeStruct((n, depth), BF16) for n in (few, many)),
        [ANY] * 4,
        [
            pltpu.VMEM(res_bands.shape, jnp.int32),
            *form_scratch[2:],
            pltpu.VMEM((rows, groups), BF16),
            pltpu.VMEM((rows, depth - groups), BF16),
            pltpu.SemaphoreType.DMA((4 + 4 * N_X * N_Z,)),
        ],
        2 * 10**9,
    )(res_pair, val_form, cond_form, res_bands)
    far, far_bands, near_bands, from_even, left_out, left_in, tables = lax.optimization_barrier(
        (far, far_bands, near_bands, from_even, left_out, left_in, tables)
    )
    from_odd = lax.ppermute(far, "blk", [(i + 1, i) for i in range(0, blocks, 2)])
    out_term, bands = call(
        out_kernel,
        "out_term",
        (jax.ShapeDtypeStruct((few // own, 2, own, cols), BF16), band_shape),
        [ANY] * 10,
        [
            block,
            block,
            index,
            index,
            *form_scratch,
            pltpu.VMEM((few, depth), BF16),
            band,
            pltpu.VMEM((few // own, 2, own, cols), BF16),
            pltpu.SemaphoreType.DMA((12,)),
        ],
        2 * 10**9,
    )(left_out, far, from_even, from_odd, far_bands, near_bands, *tables)
    *in_terms, own_terms = call(
        in_kernel,
        "in_term",
        (jax.ShapeDtypeStruct((len(OTHER_ROWS) - 1, 2, own, cols), BF16),) * N_X
        + (jax.ShapeDtypeStruct((N_X, 2, own, cols), BF16),),
        [ANY] * 2,
        [
            pltpu.VMEM((many, depth), BF16),
            band,
            pltpu.VMEM((many // own, 2, own, cols), BF16),
            pltpu.SemaphoreType.DMA((2,)),
            pltpu.SemaphoreType.DMA((2 * N_X,)),
        ],
        2 * 10**9,
    )(left_in, bands)

    to_2 = jnp.sum(shares_over_x(out_term).astype(F32), axis=0).astype(BF16)
    from_2 = along_z(to_2, 2)
    own_share, _ = lax.optimization_barrier((in_terms[0], to_2))
    shares = [own_share] + [along_x(in_terms[by], by) for by in (1, 3, 2)]

    def summed(k):
        return sum(s[k].astype(F32) for s in shares)

    to_1, to_3 = summed(0).astype(BF16), summed(1).astype(BF16)
    from_1 = along_z(to_1, 1)
    from_3 = along_z(to_3, 3)
    own_terms, _, _ = lax.optimization_barrier((own_terms, to_1, to_3))
    total = jnp.sum(shares_over_x(own_terms).astype(F32), axis=0)
    taken = pl.pallas_call(
        taken_kernel,
        in_specs=[VMEM] * 3,
        out_specs=VMEM,
        out_shape=jax.ShapeDtypeStruct(from_2.shape, F32),
        compiler_params=pltpu.CompilerParams(vmem_limit_bytes=4 * 2**20),
        cost_estimate=pl.CostEstimate(flops=8000000000, bytes_accessed=10**6, transcendentals=0),
        name="taken",
    )(from_2, from_3, from_1)
    return total + taken


def solution(mesh):
    return jax.shard_map(
        local,
        mesh=mesh,
        in_specs=(
            P("blk", "pw"),
            P("blk", "pw"),
            P("pw"),
            P("pw"),
            P(None, "pw"),
            P(None, "pw"),
            P(None, "blk"),
            P(None, "blk"),
        ),
        out_specs=P(None, ("blk", "pw"), None),
        check_vma=False,
    )
```

```python
import functools

import jax
import jax.numpy as jnp
from jax import lax
from jax.experimental import pallas as pl
from jax.experimental.pallas import tpu as pltpu
from jax.sharding import PartitionSpec as P

NV = 200
NC = 300
N_X = 4
N_Z = 4
X_GROUPS = [[x * N_Z + z for x in range(N_X)] for z in range(N_Z)]
F32 = jnp.float32
BF16 = jnp.bfloat16
VMEM_LIMIT = 63 * 2**20
ANY = pl.BlockSpec(memory_space=pl.ANY)
VMEM = pl.BlockSpec(memory_space=pltpu.VMEM)
FIRST_ROWS = (2,)
OTHER_ROWS = (1, 3)
OWN_ROWS = (0,)


def along_z(x, by):
    pairs = [(a * N_Z + z, a * N_Z + (z + by) % N_Z) for a in range(N_X) for z in range(N_Z)]
    return lax.ppermute(x, "pw", pairs)


def call(kernel, name, out_shape, in_specs, scratch, flops):
    return pl.pallas_call(
        kernel,
        in_specs=in_specs,
        out_specs=jax.tree.map(lambda _: ANY, out_shape),
        out_shape=out_shape,
        scratch_shapes=scratch,
        compiler_params=pltpu.CompilerParams(vmem_limit_bytes=VMEM_LIMIT),
        cost_estimate=pl.CostEstimate(flops=flops, bytes_accessed=10**6, transcendentals=0),
        name=name,
    )


def picked_rows(form, rows):
    hits = lax.broadcasted_iota(jnp.int32, (rows.shape[0], form.shape[0]), 1) == rows
    return jnp.dot(hits.astype(F32).astype(BF16), form, preferred_element_type=F32)


def density(rows_val, rows_cond, val_form, cond_form):
    rows = jnp.concatenate([rows_val, rows_cond] * 4, axis=0).T
    picked = picked_rows(val_form, rows[:, 0:1]) * picked_rows(cond_form, rows[:, 1:2])
    return picked.astype(BF16)


def res_kernel(
    pair_ref, val_ref, cond_ref, bands_ref, out_ref, in_ref, own_ref, bands, val, cond, pair, dens,
    sems,
):
    rows, groups = pair.shape
    own = rows // (N_X * N_Z)
    pw = lax.axis_index("pw")
    my_x, my_z = pw // N_Z, pw % N_Z
    tables = table_copies((bands_ref, val_ref, cond_ref), (bands, val, cond), sems, 0)
    for copy in tables:
        copy.start()
    read = pltpu.make_async_copy(pair_ref, pair, sems.at[3])
    read.start()
    for copy in tables:
        copy.wait()
    rows_val = bands[2:3, :] * NV + bands[0:1, :]
    rows_cond = bands[2:3, :] * NC + bands[1:2, :]
    half = rows // 2
    dens[:half, :] = density(rows_val[:, :half], rows_cond[:, :half], val[...], cond[...])
    read.wait()
    gives = []
    later = []
    for ref, steps in ((out_ref, FIRST_ROWS), (in_ref, OTHER_ROWS), (own_ref, OWN_ROWS)):
        for x in range(N_X):
            for k, m in enumerate(steps):
                owner_x = (x + my_x) % N_X if ref is in_ref else x
                owner = owner_x * N_Z + (my_z + m) % N_Z
                source = pl.ds(pl.multiple_of(owner * own, own), own)
                target = ref.at[pl.ds((x * len(steps) + k) * own, own), :]
                at = 4 + 2 * len(gives)
                gives.append(
                    pltpu.make_async_copy(
                        pair.at[source, :], target.at[:, pl.ds(0, groups)], sems.at[at]
                    )
                )
                gives[-1].start()
                later.append(
                    pltpu.make_async_copy(
                        dens.at[source, :],
                        target.at[:, pl.ds(groups, dens.shape[1])],
                        sems.at[at + 1],
                    )
                )
    dens[half:, :] = density(rows_val[:, half:], rows_cond[:, half:], val[...], cond[...])
    for give in later:
        give.start()
    for give in gives + later:
        give.wait()


def table_copies(refs, places, sems, first):
    return [
        pltpu.make_async_copy(ref, place, sems.at[first + k])
        for k, (ref, place) in enumerate(zip(refs, places, strict=True))
    ]


def product(left, right):
    return lax.dot_general(
        left, right, (((1,), (1,)), ((), ())), preferred_element_type=F32
    ).astype(BF16)


def out_kernel(
    left_ref, far_ref, even_ref, from_odd_ref, far_bands_ref, near_bands_ref,
    coulomb_ref, screening_ref, val_ref, cond_ref, out_ref, band_ref, near, far, near_bands,
    far_bands, coulomb, screening, val, cond, left, band, out, sems,
):
    cols, groups = near.shape

    odd = lax.axis_index("blk") % 2

    @pl.when(odd == 0)
    def _():
        pltpu.make_async_copy(from_odd_ref, near, sems.at[0]).start()

    @pl.when(odd != 0)
    def _():
        pltpu.make_async_copy(even_ref, near, sems.at[0]).start()

    refs = (far_ref, coulomb_ref, screening_ref, val_ref, cond_ref)
    copies = table_copies(refs, (far, coulomb, screening, val, cond), sems, 1)
    copies += table_copies((near_bands_ref, far_bands_ref), (near_bands, far_bands), sems, 10)
    for copy in copies:
        copy.start()
    rows = pltpu.make_async_copy(left_ref, left, sems.at[6])
    rows.start()
    pltpu.make_async_copy(from_odd_ref, near, sems.at[0]).wait()
    for copy in copies:
        copy.wait()
    bands = jnp.concatenate([near_bands[...], far_bands[...]], axis=1)
    rows_val = bands[2:3, :] * NV + bands[0:1, :]
    rows_cond = bands[2:3, :] * NC + bands[1:2, :]
    dens = density(rows_val, rows_cond, val[...], cond[...])
    band[:, groups:] = -((dens.astype(F32) * screening[...][None, :]).astype(BF16))
    for k, payload in enumerate((near, far)):
        weighted = (payload[...].astype(F32) * coulomb[...][None, :]).astype(BF16)
        band[k * cols : (k + 1) * cols, :groups] = weighted * 2
    keep = pltpu.make_async_copy(band, band_ref, sems.at[0])
    keep.start()
    rows.wait()
    half = out.shape[0] // 2
    halves = (out_ref.at[pl.ds(0, half)], out_ref.at[pl.ds(half, half)])
    give_product(left, band, out, halves, sems)
    keep.wait()


def give_product(left, band, out, out_refs, sems):
    gives = []
    count, steps, own, cols = out.shape
    each = count // len(out_refs)
    for k, ref in enumerate(out_refs):
        total = product(left[pl.ds(k * each * own, each * own), :], band[...])
        for n in range(each):
            for step in range(steps):
                out[k * each + n, step] = total[
                    n * own : (n + 1) * own, step * cols : (step + 1) * cols
                ]
        gives.append(pltpu.make_async_copy(out.at[pl.ds(k * each, each)], ref, sems.at[1 + k]))
        gives[-1].start()
    for give in gives:
        give.wait()


def in_kernel(left_ref, band_ref, out_0, out_1, out_2, out_3, left, band, out, sems, out_sems):
    rows = table_copies((left_ref, band_ref), (left, band), sems, 0)
    for copy in rows:
        copy.start()
    for copy in rows:
        copy.wait()
    count, steps, own, cols = out.shape
    each = count // N_X
    gives = []
    for by, ref in ((1, out_1), (3, out_3), (2, out_2), (0, out_0)):
        total = product(left[pl.ds(by * each * own, each * own), :], band[...])
        for n in range(each):
            for step in range(steps):
                out[by * each + n, step] = total[
                    n * own : (n + 1) * own, step * cols : (step + 1) * cols
                ]
        gives.append(
            pltpu.make_async_copy(out.at[pl.ds(by * each, each)], ref, out_sems.at[by])
        )
        gives[-1].start()
    for give in gives:
        give.wait()


def own_kernel(left_ref, band_ref, out_ref, left, band, out, sems):
    rows = table_copies((left_ref, band_ref), (left, band), sems, 2)
    for copy in rows:
        copy.start()
    for copy in rows:
        copy.wait()
    half = out.shape[0] // 2
    halves = (out_ref.at[pl.ds(0, half)], out_ref.at[pl.ds(half, half)])
    give_product(left, band, out, halves, sems)


def along_x(x, by):
    pairs = [(a * N_Z + z, (a + by) % N_X * N_Z + z) for a in range(N_X) for z in range(N_Z)]
    return lax.ppermute(x, "pw", pairs)


def taken_kernel(first_ref, second_ref, third_ref, out_ref):
    out_ref[...] = (
        first_ref[...].astype(F32) + second_ref[...].astype(F32) + third_ref[...].astype(F32)
    )


def shares_over_x(pieces):
    return lax.all_to_all(pieces, "pw", 0, 0, axis_index_groups=X_GROUPS)


def local(res_pair, band_pair, coulomb, screening, val_form, cond_form, res_bands, band_bands):
    rows, groups = res_pair.shape
    cols = band_pair.shape[0]
    depth = groups + val_form.shape[1]
    own = rows // (N_X * N_Z)
    few, many = (rows * len(steps) // N_Z for steps in (FIRST_ROWS, OTHER_ROWS))
    blocks = lax.axis_size("blk")
    far_on = [(i, (i + 2) % blocks) for i in range(blocks)]
    far = lax.ppermute(band_pair, "blk", far_on)
    far_bands = lax.ppermute(band_bands, "blk", far_on)
    near_bands = lax.ppermute(band_bands, "blk", [(i, (i + 1) % blocks) for i in range(blocks)])
    from_even = lax.ppermute(band_pair, "blk", [(i, i + 1) for i in range(0, blocks, 2)])

    tables = (coulomb, screening, val_form, cond_form)
    form_scratch = [pltpu.VMEM(t.shape, t.dtype) for t in tables]
    band = pltpu.VMEM((2 * cols, depth), BF16)
    block = pltpu.VMEM(band_pair.shape, BF16)
    index = pltpu.VMEM(band_bands.shape, jnp.int32)
    band_shape = jax.ShapeDtypeStruct((2 * cols, depth), BF16)
    left_out, left_in, left_own = call(
        res_kernel,
        "res_rows",
        tuple(jax.ShapeDtypeStruct((n, depth), BF16) for n in (few, many, few)),
        [ANY] * 4,
        [
            pltpu.VMEM(res_bands.shape, jnp.int32),
            *form_scratch[2:],
            pltpu.VMEM((rows, groups), BF16),
            pltpu.VMEM((rows, depth - groups), BF16),
            pltpu.SemaphoreType.DMA((4 + 4 * N_X * N_Z,)),
        ],
        2 * 10**9,
    )(res_pair, val_form, cond_form, res_bands)
    far, far_bands, near_bands, from_even, left_out, left_in, left_own, tables = lax.optimization_barrier(
        (far, far_bands, near_bands, from_even, left_out, left_in, left_own, tables)
    )
    from_odd = lax.ppermute(far, "blk", [(i + 1, i) for i in range(0, blocks, 2)])
    out_term, bands = call(
        out_kernel,
        "out_term",
        (jax.ShapeDtypeStruct((few // own, 2, own, cols), BF16), band_shape),
        [ANY] * 10,
        [
            block,
            block,
            index,
            index,
            *form_scratch,
            pltpu.VMEM((few, depth), BF16),
            band,
            pltpu.VMEM((few // own, 2, own, cols), BF16),
            pltpu.SemaphoreType.DMA((12,)),
        ],
        2 * 10**9,
    )(left_out, far, from_even, from_odd, far_bands, near_bands, *tables)
    in_terms = call(
        in_kernel,
        "in_term",
        (jax.ShapeDtypeStruct((len(OTHER_ROWS), 2, own, cols), BF16),) * N_X,
        [ANY] * 2,
        [
            pltpu.VMEM((many, depth), BF16),
            band,
            pltpu.VMEM((many // own, 2, own, cols), BF16),
            pltpu.SemaphoreType.DMA((2,)),
            pltpu.SemaphoreType.DMA((N_X,)),
        ],
        2 * 10**9,
    )(left_in, bands)

    to_2 = jnp.sum(shares_over_x(out_term).astype(F32), axis=0).astype(BF16)
    from_2 = along_z(to_2, 2)
    own_share, _ = lax.optimization_barrier((in_terms[0], to_2))
    shares = [own_share] + [along_x(in_terms[by], by) for by in (1, 3, 2)]

    def summed(k):
        return sum(s[k].astype(F32) for s in shares)

    to_1, to_3 = summed(0).astype(BF16), summed(1).astype(BF16)
    from_1 = along_z(to_1, 1)
    from_3 = along_z(to_3, 3)
    left_own, _, _ = lax.optimization_barrier((left_own, to_1, to_3))
    own_terms = call(
        own_kernel,
        "own_term",
        jax.ShapeDtypeStruct((N_X, 2, own, cols), BF16),
        [ANY] * 2,
        [
            pltpu.VMEM((few, depth), BF16),
            band,
            pltpu.VMEM((N_X, 2, own, cols), BF16),
            pltpu.SemaphoreType.DMA((4,)),
        ],
        10**8,
    )(left_own, bands)
    total = jnp.sum(shares_over_x(own_terms).astype(F32), axis=0)
    taken = pl.pallas_call(
        taken_kernel,
        in_specs=[VMEM] * 3,
        out_specs=VMEM,
        out_shape=jax.ShapeDtypeStruct(from_2.shape, F32),
        compiler_params=pltpu.CompilerParams(vmem_limit_bytes=4 * 2**20),
        cost_estimate=pl.CostEstimate(flops=8000000000, bytes_accessed=10**6, transcendentals=0),
        name="taken",
    )(from_2, from_3, from_1)
    return total + taken


def solution(mesh):
    return jax.shard_map(
        local,
        mesh=mesh,
        in_specs=(
            P("blk", "pw"),
            P("blk", "pw"),
            P("pw"),
            P("pw"),
            P(None, "pw"),
            P(None, "pw"),
            P(None, "blk"),
            P(None, "blk"),
        ),
        out_specs=P(None, ("blk", "pw"), None),
        check_vma=False,
    )
```
